512 devices in a mesh: dp: 8 (over z_lo), tm: 8 (over x, core), space: 8 (over y, z_hi).
Axes of the slice: x: 4, y: 4, z: 16 (z_hi: 2, z_lo: 8; z = z_hi * 8 + z_lo), core: 2. Of those that a mesh axis runs over, the one named last changes fastest.
Arguments:
- queries: bfloat16 [64, 1536, 3072], P(('dp', 'tm'), 'space'), parts along dimension 0, may hold values from -70 to 70
- keys: bfloat16 [64, 1536, 3072], P(('dp', 'tm'), 'space'), parts along dimension 0, may hold values from -5 to 5
- values: bfloat16 [64, 1536, 3072], P(('dp', 'tm'), 'space'), parts along dimension 0, may hold values from -6 to 6
Outputs:
- attended: bfloat16 [64, 1536, 3072], P(('dp', 'tm'), 'space'), parts along dimension 0
The draws below stay inside these ranges and needn't reach their ends.
There are 8 independent parts, one for each index of `dp`. The reference program is written for one: setup_inputs(seed, part) draws one part's arguments, and reference() takes and returns one part's arrays. A program takes and returns all parts, laid end to end along the dimension named above; each array names one. Nothing has to cross between parts.
All inputs are finite; a program needn't handle non-finite values.
Results may differ from the reference program's by a relative error of at most 0.0049.
Values may be sent and summed in bfloat16 or wider, within the bound.
No kernel may reach another device: no remote copies, remote signals or barrier semaphores. Data moves between devices by JAX's collectives and lax.ppermute only.
A program may use at most 64 MiB of HBM per device.

```python
import math
import jax
import jax.numpy as jnp
from jax import lax

HS = 16
HT = 8
DH = 128
D = 3072
FRAMES = 8
TOKENS_FRAME = 1536


def pair_fields(key, boost):
    shape = (FRAMES, TOKENS_FRAME, D)
    gauss_query = jnp.clip(jax.random.normal(jax.random.fold_in(key, 21), shape, jnp.float32), -5.0, 5.0)
    gauss_key = jnp.clip(jax.random.normal(jax.random.fold_in(key, 23), shape, jnp.float32), -5.0, 5.0)
    query = gauss_query
    keyfield = gauss_key
    strength = 12.0 + 28.0 * jax.random.uniform(jax.random.fold_in(key, 25), (FRAMES, TOKENS_FRAME, 1), jnp.float32)
    nudge = 2.0 / (strength * math.sqrt(DH))
    frame_ids = jnp.arange(FRAMES)[:, None, None]
    token_ids = jnp.arange(TOKENS_FRAME)[None, :, None]
    columns = jnp.arange(D)[None, None, :]
    spatial_col = columns < HS * DH
    chosen = token_ids % 64 == 0
    live = boost > 0.0
    target = jnp.where(spatial_col, jnp.roll(keyfield, -1, axis=1), jnp.roll(keyfield, -1, axis=0))
    aligned = jnp.where(spatial_col, chosen, chosen & (frame_ids == 0))
    query = jnp.where(aligned & live, strength * boost * target, query)
    twin_space = (token_ids % 64 == 2) & spatial_col & live
    twin_time = (frame_ids == 2) & chosen & jnp.logical_not(spatial_col) & live
    space_copy = (1.0 - jnp.roll(nudge, 2, axis=1)) * jnp.roll(keyfield, 1, axis=1)
    time_copy = (1.0 - jnp.roll(nudge, 2, axis=0)) * jnp.roll(keyfield, 1, axis=0)
    newkey = jnp.where(twin_space, space_copy, keyfield)
    newkey = jnp.where(twin_time, time_copy, newkey)
    return (query, newkey)


def draw_queries(key, part):
    query, unused_key = pair_fields(key, 0.0)
    return query.astype(jnp.bfloat16)


def draw_keys(key, part):
    unused_query, keyfield = pair_fields(key, 0.0)
    return keyfield.astype(jnp.bfloat16)


def level_of(own_key, extent, shards, smallest, largest):
    def one(axis_at, shards_of):
        draws = jax.random.uniform(jax.random.fold_in(jax.random.fold_in(own_key, 6), axis_at), (shards_of,), jnp.float32, smallest / len(shards), largest / len(shards))
        return jnp.repeat(jnp.exp(draws), extent[axis_at] // shards_of).reshape((-1,) + (1,) * (len(extent) - axis_at - 1))

    gain = one(*shards[0])
    for cut in shards[1:]:
        gain = gain * one(*cut)
    return gain


def scatter_about(rng, extent, spread, reach, cuts=(), dtype=jnp.bfloat16):
    array = jax.random.normal(rng, extent, jnp.float32) * spread
    if len(cuts) > 0:
        array = level_of(rng, extent, cuts, -0.22, 0.18) * array
    return jnp.clip(array, min=-reach, max=reach).astype(dtype)


def setup_inputs(seed: int = 0, part: int = 0) -> dict:
    streams_of = jax.random.split(jax.random.key(seed), 4)
    own_keys = jax.random.split(jax.random.fold_in(streams_of[3], part), 4)
    return {
        "queries": draw_queries(jax.random.fold_in(jax.random.fold_in(streams_of[3], part), 71), part),
        "keys": draw_keys(jax.random.fold_in(jax.random.fold_in(streams_of[3], part), 71), part),
        "values": scatter_about(own_keys[2], (FRAMES, TOKENS_FRAME, D), 1.0, 6.0, ((0, 8), (1, 8))),
    }


def attend_frame(trio):
    query, keyset, valueset = trio
    length = query.shape[0]
    query = query.astype(jnp.float32).reshape(length, HS, DH)
    keyset = keyset.astype(jnp.float32).reshape(length, HS, DH)
    valueset = valueset.astype(jnp.float32).reshape(length, HS, DH)
    scores = jnp.einsum('qhd,khd->hqk', query, keyset) * (1.0 / math.sqrt(DH))
    weights = lax.optimization_barrier(jax.nn.softmax(scores, axis=-1).astype(jnp.bfloat16)).astype(jnp.float32)
    output = jnp.einsum('hqk,khd->qhd', weights, valueset)
    return output.reshape(length, HS * DH).astype(jnp.bfloat16)

def reference(queries, keys, values):
    split = HS * DH
    spatial = lax.map(attend_frame, (queries[..., :split], keys[..., :split], values[..., :split]))
    shape = (FRAMES, TOKENS_FRAME, HT, DH)
    query_time = queries[..., split:].astype(jnp.float32).reshape(shape)
    key_time = keys[..., split:].astype(jnp.float32).reshape(shape)
    value_time = values[..., split:].astype(jnp.float32).reshape(shape)
    scores = jnp.einsum('fshd,gshd->shfg', query_time, key_time) * (1.0 / math.sqrt(DH))
    weights = lax.optimization_barrier(jax.nn.softmax(scores, axis=-1).astype(jnp.bfloat16)).astype(jnp.float32)
    temporal = jnp.einsum('shfg,gshd->fshd', weights, value_time)
    temporal = temporal.reshape(FRAMES, TOKENS_FRAME, HT * DH).astype(jnp.bfloat16)
    return jnp.concatenate([spatial, temporal], axis=-1)
```

```python
import math

import jax
import jax.numpy as jnp
from jax import lax
from jax.experimental import pallas as pl
from jax.experimental.pallas import tpu as pltpu
from jax.sharding import Mesh, PartitionSpec as P

HS = 16
HT = 8
DH = 128
Y = 4
CH = HS // Y
SCALE = 1.0 / math.sqrt(DH)
SCALE2 = SCALE * math.log2(math.e)
ANY = pl.BlockSpec(memory_space=pl.ANY)
VMEM_LIMIT = 60 * 1024 * 1024
COST = pl.CostEstimate(flops=0, bytes_accessed=0, transcendentals=0)


def params(limit=VMEM_LIMIT):
    return pltpu.CompilerParams(vmem_limit_bytes=limit)


def whole(shape):
    return pl.BlockSpec(shape, lambda i: (0,) * len(shape))


def pack(sources, out_shapes, plan, after=()):
    rows, count, skip = sources[0][0].shape[1], len(sources), len(after)

    def body(*refs):
        for source, y, o, index in plan:
            refs[count + skip + o][index] = refs[source][0, :, pl.ds(y * DH, DH)]

    return pl.pallas_call(
        body,
        grid=(1,),
        out_shape=[jax.ShapeDtypeStruct(s, jnp.bfloat16) for s in out_shapes],
        in_specs=[
            pl.BlockSpec((1, rows, Y * DH), lambda i, g=group: (0, 0, g)) for _, group in sources
        ]
        + [ANY] * skip,
        out_specs=[whole(s) for s in out_shapes],
        compiler_params=params(),
        cost_estimate=COST,
    )(*[array for array, _ in sources], *after)


def unpack(pieces, plan, rows, width, base=None):
    count = len(pieces)
    extra = 0 if base is None else 1
    groups = [group for group, _ in plan]

    def column(i):
        place = jnp.int32(groups[0])
        for n, group in enumerate(groups):
            place = jnp.where(i == n, group, place)
        return place

    def body(*refs):
        out = refs[count + extra]
        for n, (_, heads) in enumerate(plan):

            @pl.when(pl.program_id(0) == n)
            def _write(heads=heads):
                for y, (p, index) in enumerate(heads):
                    out[0, :, pl.ds(y * DH, DH)] = refs[p][index]

    return pl.pallas_call(
        body,
        grid=(len(plan),),
        out_shape=jax.ShapeDtypeStruct((1, rows, width), jnp.bfloat16),
        in_specs=[whole(p.shape) for p in pieces] + [ANY] * extra,
        out_specs=pl.BlockSpec((1, rows, Y * DH), lambda i: (0, 0, column(i))),
        input_output_aliases={} if base is None else {count: 0},
        compiler_params=params(),
        cost_estimate=COST,
    )(*pieces, *([] if base is None else [base]))


def scores_of(q, k):
    return lax.dot_general(q, k, (((1,), (1,)), ((), ())), preferred_element_type=jnp.float32)


def attend_body(q_ref, kl_ref, vl_ref, kr_ref, vr_ref, *rest):
    o_ref = rest[-1]
    rows = q_ref.shape[2]

    def flat(ref):
        return ref[...].reshape(Y * rows, DH)

    q = q_ref[0, 0]
    sl = scores_of(q, flat(kl_ref))
    sr = scores_of(q, flat(kr_ref))
    top = jnp.maximum(sl.max(axis=-1, keepdims=True), sr.max(axis=-1, keepdims=True))
    wl = jnp.exp2((sl - top) * SCALE2)
    wr = jnp.exp2((sr - top) * SCALE2)
    total = wl.sum(axis=-1, keepdims=True) + wr.sum(axis=-1, keepdims=True)
    out = jnp.dot(wl.astype(jnp.bfloat16), flat(vl_ref), preferred_element_type=jnp.float32)
    out += jnp.dot(wr.astype(jnp.bfloat16), flat(vr_ref), preferred_element_type=jnp.float32)
    o_ref[0, 0] = (out / total).astype(jnp.bfloat16)


def attend(query, near, far, slots, slot, base=None, after=()):
    rows = query[0].shape[2]

    def part(source, more):
        return pl.BlockSpec((Y, 1, rows, DH), lambda i: (0, source[1] + more, 0, 0))

    extra = [] if base is None else [base]
    return pl.pallas_call(
        attend_body,
        grid=(Y,),
        out_shape=jax.ShapeDtypeStruct((Y, slots, rows, DH), jnp.bfloat16),
        in_specs=[pl.BlockSpec((1, 1, rows, DH), lambda i: (i, query[1], 0, 0))]
        + [part(near, 0), part(near, 1), part(far, 0), part(far, 1)]
        + [ANY] * (len(extra) + len(after)),
        out_specs=pl.BlockSpec((1, 1, rows, DH), lambda i: (i, slot, 0, 0)),
        input_output_aliases={5: 0} if extra else {},
        compiler_params=params(),
        cost_estimate=COST,
    )(query[0], near[0], near[0], far[0], far[0], *extra, *after)


def frames_body(q_ref, k_ref, v_ref, o_ref):
    frames, _, tokens, _ = q_ref.shape
    size = frames * tokens
    s = scores_of(q_ref[:, 0].reshape(size, DH), k_ref[:, 0].reshape(size, DH))
    row = lax.broadcasted_iota(jnp.int32, (size, size), 0)
    column = lax.broadcasted_iota(jnp.int32, (size, size), 1)
    same = (row & (tokens - 1)) == (column & (tokens - 1))
    s = jnp.where(same, s, -jnp.inf)
    top = s.max(axis=-1, keepdims=True)
    w = jnp.exp2((s - top) * SCALE2)
    total = w.sum(axis=-1, keepdims=True)
    out = jnp.dot(
        w.astype(jnp.bfloat16), v_ref[:, 0].reshape(size, DH), preferred_element_type=jnp.float32
    )
    o_ref[...] = (out / total).astype(jnp.bfloat16).reshape(frames, tokens, DH)


def attend_frames(trio):
    frames, _, rows, _ = trio.shape
    tokens = 32

    def part(n):
        return pl.BlockSpec((frames, 1, tokens, DH), lambda i: (0, n, i, 0))

    return pl.pallas_call(
        frames_body,
        grid=(rows // tokens,),
        out_shape=jax.ShapeDtypeStruct((frames, rows, DH), jnp.bfloat16),
        in_specs=[part(0), part(1), part(2)],
        out_specs=pl.BlockSpec((frames, tokens, DH), lambda i: (0, i, 0)),
        compiler_params=pltpu.CompilerParams(vmem_limit_bytes=VMEM_LIMIT),
        cost_estimate=COST,
    )(trio, trio, trio)


def over(axis, array):
    return lax.cond(
        lax.axis_index("dp") < 8,
        lambda a: lax.all_to_all(a, axis, split_axis=0, concat_axis=0, tiled=True),
        lambda a: a,
        array,
    )


def across(array):
    return lax.ppermute(array, "zh", [(0, 1), (1, 0)])


def on_device(q, k, v):
    rows, width = q.shape[1], q.shape[2]

    (raw,) = pack(
        [(a, j) for j in (0, 1) for a in (k, v)],
        [(Y, 4, rows, DH)],
        [(n, y, 0, (y, n)) for n in range(4) for y in range(Y)],
    )
    far_raw = across(raw)
    more, trio = pack(
        [(a, j) for j in range(CH) for a in (k, v)]
        + [(q, j) for j in range(CH)]
        + [(a, CH + g) for g in range(HT // Y) for a in (q, k, v)],
        [(Y, 12, rows, DH), (HT, 3, rows, DH)],
        [(n, y, 0, (y, n)) for n in range(12) for y in range(Y)]
        + [
            (12 + g * 3 + a, y, 1, (g * Y + y, a))
            for g in range(HT // Y)
            for a in range(3)
            for y in range(Y)
        ],
        (raw,),
    )
    mixed = over("y", more)
    far23 = across(mixed[:, 4:8])
    frames_out = over("tm", attend_frames(over("tm", trio)))
    far01 = over("y", far_raw)
    out = attend((mixed, 8), (mixed, 0), (far01, 0), 2, 0)
    out = over("y", attend((mixed, 9), (mixed, 2), (far01, 2), 2, 1, out))
    early = unpack(
        [out, frames_out],
        [(j, [(0, (y, j)) for y in range(Y)]) for j in range(2)]
        + [(CH + g, [(1, g * Y + y) for y in range(Y)]) for g in range(HT // Y)],
        rows,
        width,
    )
    out = attend((mixed, 10), (mixed, 4), (far23, 0), 2, 0, after=(early,))
    out = over("y", attend((mixed, 11), (mixed, 6), (far23, 2), 2, 1, out))
    return unpack(
        [out], [(2 + j, [(0, (y, j)) for y in range(Y)]) for j in range(2)], rows, width, early
    )


def solution(mesh):
    fine = Mesh(mesh.devices.reshape(8, 8, Y, 2), ("dp", "tm", "y", "zh"))
    spec = P(("dp", "tm"), ("y", "zh"), None)
    return jax.shard_map(
        on_device, mesh=fine, in_specs=(spec, spec, spec), out_specs=spec, check_vma=False
    )
```

```python
import math

import jax
import jax.numpy as jnp
from jax import lax
from jax.experimental import pallas as pl
from jax.experimental.pallas import tpu as pltpu
from jax.sharding import Mesh, PartitionSpec as P

HS = 16
HT = 8
DH = 128
Y = 4
SCALE = 1.0 / math.sqrt(DH)
SCALE2 = SCALE * math.log2(math.e)
ANY = pl.BlockSpec(memory_space=pl.ANY)
PARAMS = pltpu.CompilerParams(vmem_limit_bytes=60 * 1024 * 1024)
COST = pl.CostEstimate(flops=0, bytes_accessed=0, transcendentals=0)


def whole(shape):
    return pl.BlockSpec(shape, lambda *_: (0,) * len(shape))


def pack(half, sources, out_shapes, plan, after=()):
    rows, count, skip = sources[0][0].shape[1], len(sources), len(after)

    def body(half_ref, *refs):
        for source, y, o, index in plan:
            refs[count + skip + o][index] = refs[source][0, :, pl.ds(y * DH, DH)]

    def column(group):
        return lambda i, half_ref: (0, 0, group[0] + group[1] * half_ref[0])

    return pl.pallas_call(
        body,
        grid_spec=pltpu.PrefetchScalarGridSpec(
            num_scalar_prefetch=1,
            grid=(1,),
            in_specs=[pl.BlockSpec((1, rows, Y * DH), column(g)) for _, g in sources] + [ANY] * skip,
            out_specs=[whole(s) for s in out_shapes],
        ),
        out_shape=[jax.ShapeDtypeStruct(s, jnp.bfloat16) for s in out_shapes],
        compiler_params=PARAMS,
        cost_estimate=COST,
    )(half, *[array for array, _ in sources], *after)


def unpack(half, pieces, plan, rows, width, base=None):
    count = len(pieces)
    extra = [] if base is None else [base]

    def column(i, half_ref):
        place = jnp.int32(0)
        for n, ((a, b), _) in enumerate(plan):
            place = jnp.where(i == n, a + b * half_ref[0], place)
        return (0, 0, place)

    def body(half_ref, *refs):
        out = refs[count + len(extra)]
        for n, (_, heads) in enumerate(plan):

            @pl.when(pl.program_id(0) == n)
            def _write(heads=heads):
                for y, (p, index) in enumerate(heads):
                    out[0, :, pl.ds(y * DH, DH)] = refs[p][index]

    return pl.pallas_call(
        body,
        grid_spec=pltpu.PrefetchScalarGridSpec(
            num_scalar_prefetch=1,
            grid=(len(plan),),
            in_specs=[whole(p.shape) for p in pieces] + [ANY] * len(extra),
            out_specs=pl.BlockSpec((1, rows, Y * DH), column),
        ),
        out_shape=jax.ShapeDtypeStruct((1, rows, width), jnp.bfloat16),
        input_output_aliases={1 + count: 0} if extra else {},
        compiler_params=PARAMS,
        cost_estimate=COST,
    )(half, *pieces, *extra)


def scores_of(q, k):
    return lax.dot_general(q, k, (((1,), (1,)), ((), ())), preferred_element_type=jnp.float32)


def attend_body(q0_ref, q1_ref, kl_ref, vl_ref, kr_ref, vr_ref, *rest):
    o_ref = rest[-1]
    rows = q0_ref.shape[2]

    def flat(ref):
        return ref[...].reshape(Y * rows, DH)

    q = jnp.where(pl.program_id(0) == 0, q0_ref[0, 0], q1_ref[0, 0])
    sl = scores_of(q, flat(kl_ref))
    sr = scores_of(q, flat(kr_ref))
    top = jnp.maximum(sl.max(axis=-1, keepdims=True), sr.max(axis=-1, keepdims=True))
    wl = jnp.exp2((sl - top) * SCALE2)
    wr = jnp.exp2((sr - top) * SCALE2)
    total = wl.sum(axis=-1, keepdims=True) + wr.sum(axis=-1, keepdims=True)
    out = jnp.dot(wl.astype(jnp.bfloat16), flat(vl_ref), preferred_element_type=jnp.float32)
    out += jnp.dot(wr.astype(jnp.bfloat16), flat(vr_ref), preferred_element_type=jnp.float32)
    o_ref[0, 0] = (out / total).astype(jnp.bfloat16)


def attend(queries, near, far, step, after=()):
    (q0, s0), (q1, s1) = queries
    rows = q0.shape[2]

    def part(slot):
        return pl.BlockSpec((Y, 1, rows, DH), lambda n, i: (0, slot + step * n, 0, 0))

    return pl.pallas_call(
        attend_body,
        grid=(2, Y),
        out_shape=jax.ShapeDtypeStruct((Y, 2, rows, DH), jnp.bfloat16),
        in_specs=[
            pl.BlockSpec((1, 1, rows, DH), lambda n, i: (jnp.where(n == 0, i, Y - 1), s0, 0, 0)),
            pl.BlockSpec((1, 1, rows, DH), lambda n, i: (jnp.where(n == 1, i, 0), s1, 0, 0)),
            part(near[1]),
            part(near[1] + 1),
            part(far[1]),
            part(far[1] + 1),
        ]
        + [ANY] * len(after),
        out_specs=pl.BlockSpec((1, 1, rows, DH), lambda n, i: (i, n, 0, 0)),
        compiler_params=PARAMS,
        cost_estimate=COST,
    )(q0, q1, near[0], near[0], far[0], far[0], *after)


def frames_body(q_ref, k_ref, v_ref, o_ref):
    frames, _, tokens, _ = q_ref.shape
    size = frames * tokens
    s = scores_of(q_ref[:, 0].reshape(size, DH), k_ref[:, 0].reshape(size, DH))
    row = lax.broadcasted_iota(jnp.int32, (size, size), 0)
    column = lax.broadcasted_iota(jnp.int32, (size, size), 1)
    same = (row & (tokens - 1)) == (column & (tokens - 1))
    s = jnp.where(same, s, -jnp.inf)
    top = s.max(axis=-1, keepdims=True)
    w = jnp.exp2((s - top) * SCALE2)
    total = w.sum(axis=-1, keepdims=True)
    out = jnp.dot(
        w.astype(jnp.bfloat16), v_ref[:, 0].reshape(size, DH), preferred_element_type=jnp.float32
    )
    o_ref[...] = (out / total).astype(jnp.bfloat16).reshape(frames, tokens, DH)


def attend_frames(trio):
    frames, _, rows, _ = trio.shape
    tokens = 32

    def part(n):
        return pl.BlockSpec((frames, 1, tokens, DH), lambda i: (0, n, i, 0))

    return pl.pallas_call(
        frames_body,
        grid=(rows // tokens,),
        out_shape=jax.ShapeDtypeStruct((frames, rows, DH), jnp.bfloat16),
        in_specs=[part(0), part(1), part(2)],
        out_specs=pl.BlockSpec((frames, tokens, DH), lambda i: (0, i, 0)),
        compiler_params=PARAMS,
        cost_estimate=COST,
    )(trio, trio, trio)


def over(axis, array):
    return lax.cond(
        lax.axis_index("dp") < 8,
        lambda a: lax.all_to_all(a, axis, split_axis=0, concat_axis=0, tiled=True),
        lambda a: a,
        array,
    )


def across(array):
    return lax.ppermute(array, "zh", [(0, 1), (1, 0)])


def on_device(q, k, v):
    rows, width = q.shape[1], q.shape[2]
    half = lax.axis_index("zh").astype(jnp.int32).reshape(1)
    (raw,) = pack(
        half,
        [(a, (3, -1)) for a in (q, k, v)],
        [(Y, 3, rows, DH)],
        [(n, y, 0, (y, n)) for n in range(3) for y in range(Y)],
    )
    far_raw = across(raw)
    more, trio = pack(
        half,
        [(a, (2, 1)) for a in (q, k, v)]
        + [(a, (j, 0)) for j in range(2) for a in (k, v)]
        + [(q, (j, 0)) for j in range(2)]
        + [(a, (HS // Y + g, 0)) for g in range(HT // Y) for a in (q, k, v)],
        [(Y, 9, rows, DH), (HT, 3, rows, DH)],
        [(n, y, 0, (y, n)) for n in range(9) for y in range(Y)]
        + [
            (9 + g * 3 + a, y, 1, (g * Y + y, a))
            for g in range(HT // Y)
            for a in range(3)
            for y in range(Y)
        ],
        (raw,),
    )
    mixed = over("y", more)
    far_pairs = across(mixed[:, 3:7])
    frames_out = over("tm", attend_frames(over("tm", trio)))
    far = over("y", far_raw)
    own = over("y", attend([(mixed, 0), (far, 0)], (mixed, 1), (far, 1), 0, (frames_out,)))
    back = across(own[:, 1])
    early = unpack(
        half,
        [own, frames_out],
        [((2, 1), [(0, (y, 0)) for y in range(Y)])]
        + [((HS // Y + g, 0), [(1, g * Y + y) for y in range(Y)]) for g in range(HT // Y)],
        rows,
        width,
    )
    pairs = over(
        "y", attend([(mixed, 7), (mixed, 8)], (mixed, 3), (far_pairs, 0), 2, (early,))
    )
    return unpack(
        half,
        [pairs, back],
        [((j, 0), [(0, (y, j)) for y in range(Y)]) for j in range(2)]
        + [((3, -1), [(1, y) for y in range(Y)])],
        rows,
        width,
        early,
    )


def solution(mesh):
    fine = Mesh(mesh.devices.reshape(8, 8, Y, 2), ("dp", "tm", "y", "zh"))
    spec = P(("dp", "tm"), ("y", "zh"), None)
    return jax.shard_map(
        on_device, mesh=fine, in_specs=(spec, spec, spec), out_specs=spec, check_vma=False
    )
```

```python
import functools
import math

import jax
import jax.numpy as jnp
from jax import lax
from jax.experimental import pallas as pl
from jax.experimental.pallas import tpu as pltpu
from jax.sharding import Mesh, PartitionSpec as P

HS = 16
HT = 8
DH = 128
Y = 4
SCALE = 1.0 / math.sqrt(DH)
SCALE2 = SCALE * math.log2(math.e)
ANY = pl.BlockSpec(memory_space=pl.ANY)
PARAMS = pltpu.CompilerParams(vmem_limit_bytes=66_900_000)
SMALL = pltpu.CompilerParams(vmem_limit_bytes=60 * 1024 * 1024)
COST = pl.CostEstimate(flops=0, bytes_accessed=0, transcendentals=0)


def whole(shape):
    return pl.BlockSpec(shape, lambda *_: (0,) * len(shape))


def pack(half, sources, out_shapes, plan, after=()):
    rows, count, skip = sources[0][0].shape[1], len(sources), len(after)

    def body(half_ref, *refs):
        for source, y, o, index in plan:
            refs[count + skip + o][index] = refs[source][0, :, pl.ds(y * DH, DH)]

    def column(group):
        return lambda i, half_ref: (0, 0, group[0] + group[1] * half_ref[0])

    return pl.pallas_call(
        body,
        grid_spec=pltpu.PrefetchScalarGridSpec(
            num_scalar_prefetch=1,
            grid=(1,),
            in_specs=[pl.BlockSpec((1, rows, Y * DH), column(g)) for _, g in sources] + [ANY] * skip,
            out_specs=[whole(s) for s in out_shapes],
        ),
        out_shape=[jax.ShapeDtypeStruct(s, jnp.bfloat16) for s in out_shapes],
        compiler_params=PARAMS,
        cost_estimate=COST,
    )(half, *[array for array, _ in sources], *after)


def here(ref):
    if isinstance(ref, tuple):
        return jnp.where(lax.axis_index("zh") == 0, ref[0], ref[1])
    return ref


def unpack(pieces, plan, first, rows, width, base=None):
    count = len(pieces)
    extra = [] if base is None else [base]

    def body(*refs):
        out = refs[count + len(extra)]
        for n, place in enumerate(plan):
            if isinstance(place[0], tuple):
                head = here(tuple(refs[p][index] for p, index in place))
            else:
                head = refs[place[0]][place[1]]
            out[0, :, pl.ds(n * DH, DH)] = head

    return pl.pallas_call(
        body,
        grid=(1,),
        out_shape=jax.ShapeDtypeStruct((1, rows, width), jnp.bfloat16),
        in_specs=[whole(p.shape) for p in pieces] + [ANY] * len(extra),
        out_specs=pl.BlockSpec((1, rows, len(plan) * DH), lambda i: (0, 0, first // len(plan))),
        input_output_aliases={count: 0} if extra else {},
        compiler_params=PARAMS,
        cost_estimate=COST,
    )(*pieces, *extra)


def scores_of(q, k):
    return lax.dot_general(q, k, (((1,), (1,)), ((), ())), preferred_element_type=jnp.float32)


def attend_body(jobs, *refs):
    o_ref = refs[-1]
    _, _, rows, _ = o_ref.shape
    size, parts = Y * rows, 2
    step = size // parts

    def flat(n):
        return refs[n][...].reshape(size, DH)

    def scores(task):
        q, kl, _, kr, _ = jobs[task // parts]
        query = flat(q)[task % parts * step : (task % parts + 1) * step]
        return scores_of(query, flat(kl)), scores_of(query, flat(kr))

    def weigh(w, n):
        both = jnp.concatenate([flat(n), jnp.ones((size, DH), jnp.bfloat16)], axis=-1)
        return jnp.dot(w.astype(jnp.bfloat16), both, preferred_element_type=jnp.float32)

    tasks = len(jobs) * parts
    ahead, outs = scores(0), []
    for task in range(tasks):
        (sl, sr), ahead = ahead, scores(task + 1) if task + 1 < tasks else None
        top = jnp.maximum(sl.max(axis=-1, keepdims=True), sr.max(axis=-1, keepdims=True))
        _, _, vl, _, vr = jobs[task // parts]
        out = weigh(jnp.exp2((sl - top) * SCALE2), vl) + weigh(jnp.exp2((sr - top) * SCALE2), vr)
        outs.append((out[:, :DH] / out[:, DH:]).astype(jnp.bfloat16))
    for n in range(len(jobs)):
        o_ref[:, n] = jnp.concatenate(outs[n * parts : (n + 1) * parts]).reshape(Y, rows, DH)


def attend(jobs, slots, slot=0, base=None, after=(), limit=PARAMS):
    operands, indices = [], []

    def use(array, n):
        for m, (other, k) in enumerate(operands):
            if other is array and k == n:
                return m
        operands.append((array, n))
        return len(operands) - 1

    for (q, sq), (near, sn), (far, sf) in jobs:
        indices.append((use(q, sq), use(near, sn), use(near, sn + 1), use(far, sf), use(far, sf + 1)))
    rows = jobs[0][0][0].shape[2]
    extra = [] if base is None else [base]
    return pl.pallas_call(
        functools.partial(attend_body, indices),
        grid=(1,),
        out_shape=jax.ShapeDtypeStruct((Y, slots, rows, DH), jnp.bfloat16),
        in_specs=[
            pl.BlockSpec((Y, 1, rows, DH), lambda i, n=n: (0, n, 0, 0)) for _, n in operands
        ]
        + [ANY] * (len(extra) + len(after)),
        out_specs=pl.BlockSpec(
            (Y, len(jobs), rows, DH), lambda i: (0, slot // len(jobs), 0, 0)
        ),
        input_output_aliases={len(operands): 0} if extra else {},
        compiler_params=limit,
        cost_estimate=COST,
    )(*[array for array, _ in operands], *extra, *after)


def take(array, first, count, after=()):
    _, _, rows, _ = array.shape

    def body(i_ref, *refs):
        refs[-1][...] = i_ref[...]

    return pl.pallas_call(
        body,
        grid=(Y,),
        out_shape=jax.ShapeDtypeStruct((Y, count, rows, DH), jnp.bfloat16),
        in_specs=[pl.BlockSpec((1, count, rows, DH), lambda i: (i, first // count, 0, 0))]
        + [ANY] * len(after),
        out_specs=pl.BlockSpec((1, count, rows, DH), lambda i: (i, 0, 0, 0)),
        compiler_params=PARAMS,
        cost_estimate=COST,
    )(array, *after)


def frames_body(q_ref, k_ref, v_ref, o_ref):
    frames, _, tokens, _ = q_ref.shape
    size = frames * tokens
    s = scores_of(q_ref[:, 0].reshape(size, DH), k_ref[:, 0].reshape(size, DH))
    row = lax.broadcasted_iota(jnp.int32, (size, size), 0)
    column = lax.broadcasted_iota(jnp.int32, (size, size), 1)
    same = (row & (tokens - 1)) == (column & (tokens - 1))
    s = jnp.where(same, s, -jnp.inf)
    top = s.max(axis=-1, keepdims=True)
    w = jnp.exp2((s - top) * SCALE2)
    total = w.sum(axis=-1, keepdims=True)
    out = jnp.dot(
        w.astype(jnp.bfloat16), v_ref[:, 0].reshape(size, DH), preferred_element_type=jnp.float32
    )
    o_ref[...] = (out / total).astype(jnp.bfloat16).reshape(frames, tokens, DH)


def attend_frames(trio):
    frames, _, rows, _ = trio.shape
    tokens = 32

    def part(n):
        return pl.BlockSpec((frames, 1, tokens, DH), lambda i: (0, n, i, 0))

    return pl.pallas_call(
        frames_body,
        grid=(rows // tokens,),
        out_shape=jax.ShapeDtypeStruct((frames, rows, DH), jnp.bfloat16),
        in_specs=[part(0), part(1), part(2)],
        out_specs=pl.BlockSpec((frames, tokens, DH), lambda i: (0, i, 0)),
        compiler_params=PARAMS,
        cost_estimate=COST,
    )(trio, trio, trio)


def over(axis, array):
    return lax.cond(
        lax.axis_index("dp") < 8,
        lambda a: lax.all_to_all(a, axis, split_axis=0, concat_axis=0, tiled=True),
        jnp.zeros_like,
        array,
    )


def across(array):
    return lax.ppermute(array, "zh", [(0, 1), (1, 0)])


def on_device(q, k, v):
    rows, width = q.shape[1], q.shape[2]
    half = lax.axis_index("zh").astype(jnp.int32).reshape(1)
    (raw,) = pack(
        half,
        [(a, (3, -1)) for a in (q, k, v)],
        [(Y, 3, rows, DH)],
        [(n, y, 0, (y, n)) for n in range(3) for y in range(Y)],
    )
    far_raw = across(raw)
    more, trio = pack(
        half,
        [(a, (j, 0)) for j in range(2) for a in (k, v)]
        + [(q, (j, 0)) for j in range(2)]
        + [(a, (2, 1)) for a in (q, k, v)]
        + [(a, (HS // Y + g, 0)) for g in range(HT // Y) for a in (q, k, v)],
        [(Y, 9, rows, DH), (HT, 3, rows, DH)],
        [(n, y, 0, (y, n)) for n in range(9) for y in range(Y)]
        + [
            (9 + g * 3 + a, y, 1, (g * Y + y, a))
            for g in range(HT // Y)
            for a in range(3)
            for y in range(Y)
        ],
        (raw,),
    )
    mixed = over("y", more)
    far01 = across(take(mixed, 0, 4))
    frames_out = over("tm", attend_frames(over("tm", trio)))
    early = unpack([frames_out], [(0, h) for h in range(HT)], HS, rows, width)
    far = over("y", far_raw)
    own = over(
        "y",
        attend(
            [((mixed, 6), (mixed, 7), (far, 1)), ((far, 0), (mixed, 7), (far, 1))], 2, after=(early,), limit=SMALL
        ),
    )
    back = across(own[:, 1])
    jobs = [((mixed, 4 + j), (mixed, 2 * j), (far01, 2 * j)) for j in range(2)]
    pairs = over("y", attend(jobs, 2, after=(own,), limit=SMALL))
    return unpack(
        [pairs, own, back],
        [(0, (y, j)) for j in range(2) for y in range(Y)]
        + [((1, (y, 0)), (2, y)) for y in range(Y)]
        + [((2, y), (1, (y, 0))) for y in range(Y)],
        0,
        rows,
        width,
        early,
    )


def solution(mesh):
    fine = Mesh(mesh.devices.reshape(8, 8, Y, 2), ("dp", "tm", "y", "zh"))
    spec = P(("dp", "tm"), ("y", "zh"), None)
    return jax.shard_map(
        on_device, mesh=fine, in_specs=(spec, spec, spec), out_specs=spec, check_vma=False
    )
```

```python
import functools
import math

import jax
import jax.numpy as jnp
from jax import lax
from jax.experimental import pallas as pl
from jax.experimental.pallas import tpu as pltpu
from jax.sharding import Mesh, PartitionSpec as P

HS = 16
HT = 8
DH = 128
Y = 4
SCALE = 1.0 / math.sqrt(DH)
SCALE2 = SCALE * math.log2(math.e)
ANY = pl.BlockSpec(memory_space=pl.ANY)
PARAMS = pltpu.CompilerParams(vmem_limit_bytes=60 * 1024 * 1024)
COST = pl.CostEstimate(flops=0, bytes_accessed=0, transcendentals=0)


def whole(shape):
    return pl.BlockSpec(shape, lambda *_: (0,) * len(shape))


def pack(half, sources, out_shapes, plan, after=()):
    rows, count, skip = sources[0][0].shape[1], len(sources), len(after)

    def body(half_ref, *refs):
        for source, y, o, index in plan:
            refs[count + skip + o][index] = refs[source][0, :, pl.ds(y * DH, DH)]

    def column(group):
        return lambda i, half_ref: (0, 0, group[0] + group[1] * half_ref[0])

    return pl.pallas_call(
        body,
        grid_spec=pltpu.PrefetchScalarGridSpec(
            num_scalar_prefetch=1,
            grid=(1,),
            in_specs=[pl.BlockSpec((1, rows, Y * DH), column(g)) for _, g in sources] + [ANY] * skip,
            out_specs=[whole(s) for s in out_shapes],
        ),
        out_shape=[jax.ShapeDtypeStruct(s, jnp.bfloat16) for s in out_shapes],
        compiler_params=PARAMS,
        cost_estimate=COST,
    )(half, *[array for array, _ in sources], *after)


def unpack(half, pieces, plan, rows, width, base=None):
    count = len(pieces)
    extra = [] if base is None else [base]

    def column(i, half_ref):
        place = jnp.int32(0)
        for n, ((a, b), _) in enumerate(plan):
            place = jnp.where(i == n, a + b * half_ref[0], place)
        return (0, 0, place)

    def body(half_ref, *refs):
        out = refs[count + len(extra)]
        for n, (_, heads) in enumerate(plan):

            @pl.when(pl.program_id(0) == n)
            def _write(heads=heads):
                for y, (p, index) in enumerate(heads):
                    out[0, :, pl.ds(y * DH, DH)] = refs[p][index]

    return pl.pallas_call(
        body,
        grid_spec=pltpu.PrefetchScalarGridSpec(
            num_scalar_prefetch=1,
            grid=(len(plan),),
            in_specs=[whole(p.shape) for p in pieces] + [ANY] * len(extra),
            out_specs=pl.BlockSpec((1, rows, Y * DH), column),
        ),
        out_shape=jax.ShapeDtypeStruct((1, rows, width), jnp.bfloat16),
        input_output_aliases={1 + count: 0} if extra else {},
        compiler_params=PARAMS,
        cost_estimate=COST,
    )(half, *pieces, *extra)


def scores_of(q, k):
    return lax.dot_general(q, k, (((1,), (1,)), ((), ())), preferred_element_type=jnp.float32)


def attend_body(jobs, *refs):
    o_ref = refs[-1]
    _, _, rows, _ = o_ref.shape
    size, parts = Y * rows, 2
    step = size // parts

    def flat(n):
        return refs[n][...].reshape(size, DH)

    def scores(task):
        q, kl, _, kr, _ = jobs[task // parts]
        query = flat(q)[task % parts * step : (task % parts + 1) * step]
        return scores_of(query, flat(kl)), scores_of(query, flat(kr))

    def weigh(w, n):
        both = jnp.concatenate([flat(n), jnp.ones((size, DH), jnp.bfloat16)], axis=-1)
        return jnp.dot(w.astype(jnp.bfloat16), both, preferred_element_type=jnp.float32)

    tasks = len(jobs) * parts
    ahead, outs = scores(0), []
    for task in range(tasks):
        (sl, sr), ahead = ahead, scores(task + 1) if task + 1 < tasks else None
        top = jnp.maximum(sl.max(axis=-1, keepdims=True), sr.max(axis=-1, keepdims=True))
        _, _, vl, _, vr = jobs[task // parts]
        out = weigh(jnp.exp2((sl - top) * SCALE2), vl) + weigh(jnp.exp2((sr - top) * SCALE2), vr)
        outs.append((out[:, :DH] / out[:, DH:]).astype(jnp.bfloat16))
    for n in range(len(jobs)):
        o_ref[:, n] = jnp.concatenate(outs[n * parts : (n + 1) * parts]).reshape(Y, rows, DH)


def attend(jobs, slots, slot=0, base=None, after=()):
    operands, indices = [], []

    def use(array, n):
        for m, (other, k) in enumerate(operands):
            if other is array and k == n:
                return m
        operands.append((array, n))
        return len(operands) - 1

    for (q, sq), (near, sn), (far, sf) in jobs:
        indices.append((use(q, sq), use(near, sn), use(near, sn + 1), use(far, sf), use(far, sf + 1)))
    rows = jobs[0][0][0].shape[2]
    extra = [] if base is None else [base]
    return pl.pallas_call(
        functools.partial(attend_body, indices),
        grid=(1,),
        out_shape=jax.ShapeDtypeStruct((Y, slots, rows, DH), jnp.bfloat16),
        in_specs=[
            pl.BlockSpec((Y, 1, rows, DH), lambda i, n=n: (0, n, 0, 0)) for _, n in operands
        ]
        + [ANY] * (len(extra) + len(after)),
        out_specs=pl.BlockSpec(
            (Y, len(jobs), rows, DH), lambda i: (0, slot // len(jobs), 0, 0)
        ),
        input_output_aliases={len(operands): 0} if extra else {},
        compiler_params=PARAMS,
        cost_estimate=COST,
    )(*[array for array, _ in operands], *extra, *after)


def take(array, first, count, after=()):
    _, _, rows, _ = array.shape

    def body(i_ref, *refs):
        refs[-1][...] = i_ref[...]

    return pl.pallas_call(
        body,
        grid=(Y,),
        out_shape=jax.ShapeDtypeStruct((Y, count, rows, DH), jnp.bfloat16),
        in_specs=[pl.BlockSpec((1, count, rows, DH), lambda i: (i, first // count, 0, 0))]
        + [ANY] * len(after),
        out_specs=pl.BlockSpec((1, count, rows, DH), lambda i: (i, 0, 0, 0)),
        compiler_params=PARAMS,
        cost_estimate=COST,
    )(array, *after)


def frames_body(q_ref, k_ref, v_ref, o_ref):
    frames, _, tokens, _ = q_ref.shape
    size = frames * tokens
    s = scores_of(q_ref[:, 0].reshape(size, DH), k_ref[:, 0].reshape(size, DH))
    row = lax.broadcasted_iota(jnp.int32, (size, size), 0)
    column = lax.broadcasted_iota(jnp.int32, (size, size), 1)
    same = (row & (tokens - 1)) == (column & (tokens - 1))
    s = jnp.where(same, s, -jnp.inf)
    top = s.max(axis=-1, keepdims=True)
    w = jnp.exp2((s - top) * SCALE2)
    total = w.sum(axis=-1, keepdims=True)
    out = jnp.dot(
        w.astype(jnp.bfloat16), v_ref[:, 0].reshape(size, DH), preferred_element_type=jnp.float32
    )
    o_ref[...] = (out / total).astype(jnp.bfloat16).reshape(frames, tokens, DH)


def attend_frames(trio):
    frames, _, rows, _ = trio.shape
    tokens = 32

    def part(n):
        return pl.BlockSpec((frames, 1, tokens, DH), lambda i: (0, n, i, 0))

    return pl.pallas_call(
        frames_body,
        grid=(rows // tokens,),
        out_shape=jax.ShapeDtypeStruct((frames, rows, DH), jnp.bfloat16),
        in_specs=[part(0), part(1), part(2)],
        out_specs=pl.BlockSpec((frames, tokens, DH), lambda i: (0, i, 0)),
        compiler_params=PARAMS,
        cost_estimate=COST,
    )(trio, trio, trio)


def over(axis, array):
    return lax.cond(
        lax.axis_index("dp") < 8,
        lambda a: lax.all_to_all(a, axis, split_axis=0, concat_axis=0, tiled=True),
        lambda a: a,
        array,
    )


def across(array):
    return lax.ppermute(array, "zh", [(0, 1), (1, 0)])


def on_device(q, k, v):
    rows, width = q.shape[1], q.shape[2]
    half = lax.axis_index("zh").astype(jnp.int32).reshape(1)
    (raw,) = pack(
        half,
        [(a, (3, -1)) for a in (q, k, v)],
        [(Y, 3, rows, DH)],
        [(n, y, 0, (y, n)) for n in range(3) for y in range(Y)],
    )
    far_raw = across(raw)
    more, trio = pack(
        half,
        [(a, (j, 0)) for j in range(2) for a in (k, v)]
        + [(q, (j, 0)) for j in range(2)]
        + [(a, (2, 1)) for a in (q, k, v)]
        + [(a, (HS // Y + g, 0)) for g in range(HT // Y) for a in (q, k, v)],
        [(Y, 9, rows, DH), (HT, 3, rows, DH)],
        [(n, y, 0, (y, n)) for n in range(9) for y in range(Y)]
        + [
            (9 + g * 3 + a, y, 1, (g * Y + y, a))
            for g in range(HT // Y)
            for a in range(3)
            for y in range(Y)
        ],
        (raw,),
    )
    mixed = over("y", more)
    far0 = across(take(mixed, 0, 2))
    trio = over("tm", trio)
    far1 = across(take(mixed, 2, 2, (trio,)))
    frames_out = over("tm", attend_frames(trio))
    early = unpack(
        half,
        [frames_out],
        [((HS // Y + g, 0), [(0, g * Y + y) for y in range(Y)]) for g in range(HT // Y)],
        rows,
        width,
    )
    far = over("y", far_raw)
    own = over(
        "y",
        attend(
            [((mixed, 6), (mixed, 7), (far, 1)), ((far, 0), (mixed, 7), (far, 1))], 2, after=(early,)
        ),
    )
    back = across(own[:, 1])
    pairs = attend([((mixed, 4), (mixed, 0), (far0, 0))], 2, after=(own,))
    pairs = over("y", attend([((mixed, 5), (mixed, 2), (far1, 0))], 2, 1, pairs))
    return unpack(
        half,
        [pairs, own, back],
        [((j, 0), [(0, (y, j)) for y in range(Y)]) for j in range(2)]
        + [((2, 1), [(1, (y, 0)) for y in range(Y)]), ((3, -1), [(2, y) for y in range(Y)])],
        rows,
        width,
        early,
    )


def solution(mesh):
    fine = Mesh(mesh.devices.reshape(8, 8, Y, 2), ("dp", "tm", "y", "zh"))
    spec = P(("dp", "tm"), ("y", "zh"), None)
    return jax.shard_map(
        on_device, mesh=fine, in_specs=(spec, spec, spec), out_specs=spec, check_vma=False
    )
```

```python
import functools
import math

import jax
import jax.numpy as jnp
from jax import lax
from jax.experimental import pallas as pl
from jax.experimental.pallas import tpu as pltpu
from jax.sharding import Mesh, PartitionSpec as P

HS = 16
HT = 8
DH = 128
Y = 4
SCALE = 1.0 / math.sqrt(DH)
SCALE2 = SCALE * math.log2(math.e)
ANY = pl.BlockSpec(memory_space=pl.ANY)
PARAMS = pltpu.CompilerParams(vmem_limit_bytes=60 * 1024 * 1024)
LAST = pltpu.CompilerParams(vmem_limit_bytes=66_900_000)
COST = pl.CostEstimate(flops=0, bytes_accessed=0, transcendentals=0)


def whole(shape):
    return pl.BlockSpec(shape, lambda *_: (0,) * len(shape))


def pack(half, sources, out_shapes, plan, after=()):
    rows, count, skip = sources[0][0].shape[1], len(sources), len(after)

    def body(half_ref, *refs):
        for source, y, o, index in plan:
            refs[count + skip + o][index] = refs[source][0, :, pl.ds(y * DH, DH)]

    def column(group):
        return lambda i, half_ref: (0, 0, group[0] + group[1] * half_ref[0])

    return pl.pallas_call(
        body,
        grid_spec=pltpu.PrefetchScalarGridSpec(
            num_scalar_prefetch=1,
            grid=(1,),
            in_specs=[pl.BlockSpec((1, rows, Y * DH), column(g)) for _, g in sources] + [ANY] * skip,
            out_specs=[whole(s) for s in out_shapes],
        ),
        out_shape=[jax.ShapeDtypeStruct(s, jnp.bfloat16) for s in out_shapes],
        compiler_params=PARAMS,
        cost_estimate=COST,
    )(half, *[array for array, _ in sources], *after)


def here(ref):
    if isinstance(ref, tuple):
        return jnp.where(lax.axis_index("zh") == 0, ref[0], ref[1])
    return ref


def unpack(pieces, plan, first, rows, width, base=None, limit=PARAMS):
    count = len(pieces)
    extra = [] if base is None else [base]

    def body(*refs):
        out = refs[count + len(extra)]
        for n, place in enumerate(plan):
            if isinstance(place[0], tuple):
                head = here(tuple(refs[p][index] for p, index in place))
            else:
                head = refs[place[0]][place[1]]
            out[0, :, pl.ds(n * DH, DH)] = head

    return pl.pallas_call(
        body,
        grid=(1,),
        out_shape=jax.ShapeDtypeStruct((1, rows, width), jnp.bfloat16),
        in_specs=[whole(p.shape) for p in pieces] + [ANY] * len(extra),
        out_specs=pl.BlockSpec((1, rows, len(plan) * DH), lambda i: (0, 0, first // len(plan))),
        input_output_aliases={count: 0} if extra else {},
        compiler_params=limit,
        cost_estimate=COST,
    )(*pieces, *extra)


def scores_of(q, k):
    return lax.dot_general(q, k, (((1,), (1,)), ((), ())), preferred_element_type=jnp.float32)


def attend_body(jobs, *refs):
    o_ref = refs[-1]
    _, _, rows, _ = o_ref.shape
    size, parts = Y * rows, 2
    step = size // parts

    def flat(n):
        return refs[n][...].reshape(size, DH)

    def scores(task):
        q, kl, _, kr, _ = jobs[task // parts]
        query = flat(q)[task % parts * step : (task % parts + 1) * step]
        return scores_of(query, flat(kl)), scores_of(query, flat(kr))

    def weigh(w, n):
        both = jnp.concatenate([flat(n), jnp.ones((size, DH), jnp.bfloat16)], axis=-1)
        return jnp.dot(w.astype(jnp.bfloat16), both, preferred_element_type=jnp.float32)

    tasks = len(jobs) * parts
    ahead, outs = scores(0), []
    for task in range(tasks):
        (sl, sr), ahead = ahead, scores(task + 1) if task + 1 < tasks else None
        top = jnp.maximum(sl.max(axis=-1, keepdims=True), sr.max(axis=-1, keepdims=True))
        _, _, vl, _, vr = jobs[task // parts]
        out = weigh(jnp.exp2((sl - top) * SCALE2), vl) + weigh(jnp.exp2((sr - top) * SCALE2), vr)
        outs.append((out[:, :DH] / out[:, DH:]).astype(jnp.bfloat16))
    for n in range(len(jobs)):
        o_ref[:, n] = jnp.concatenate(outs[n * parts : (n + 1) * parts]).reshape(Y, rows, DH)


def attend(jobs, slots, slot=0, base=None, after=()):
    operands, indices = [], []

    def use(array, n):
        for m, (other, k) in enumerate(operands):
            if other is array and k == n:
                return m
        operands.append((array, n))
        return len(operands) - 1

    for (q, sq), (near, sn), (far, sf) in jobs:
        indices.append((use(q, sq), use(near, sn), use(near, sn + 1), use(far, sf), use(far, sf + 1)))
    rows = jobs[0][0][0].shape[2]
    extra = [] if base is None else [base]
    return pl.pallas_call(
        functools.partial(attend_body, indices),
        grid=(1,),
        out_shape=jax.ShapeDtypeStruct((Y, slots, rows, DH), jnp.bfloat16),
        in_specs=[
            pl.BlockSpec((Y, 1, rows, DH), lambda i, n=n: (0, n, 0, 0)) for _, n in operands
        ]
        + [ANY] * (len(extra) + len(after)),
        out_specs=pl.BlockSpec(
            (Y, len(jobs), rows, DH), lambda i: (0, slot // len(jobs), 0, 0)
        ),
        input_output_aliases={len(operands): 0} if extra else {},
        compiler_params=PARAMS,
        cost_estimate=COST,
    )(*[array for array, _ in operands], *extra, *after)


def take(array, first, count, after=()):
    _, _, rows, _ = array.shape

    def body(i_ref, *refs):
        refs[-1][...] = i_ref[...]

    return pl.pallas_call(
        body,
        grid=(Y,),
        out_shape=jax.ShapeDtypeStruct((Y, count, rows, DH), jnp.bfloat16),
        in_specs=[pl.BlockSpec((1, count, rows, DH), lambda i: (i, first // count, 0, 0))]
        + [ANY] * len(after),
        out_specs=pl.BlockSpec((1, count, rows, DH), lambda i: (i, 0, 0, 0)),
        compiler_params=PARAMS,
        cost_estimate=COST,
    )(array, *after)


def frames_body(q_ref, k_ref, v_ref, o_ref):
    frames, _, tokens, _ = q_ref.shape
    size = frames * tokens
    s = scores_of(q_ref[:, 0].reshape(size, DH), k_ref[:, 0].reshape(size, DH))
    row = lax.broadcasted_iota(jnp.int32, (size, size), 0)
    column = lax.broadcasted_iota(jnp.int32, (size, size), 1)
    same = (row & (tokens - 1)) == (column & (tokens - 1))
    s = jnp.where(same, s, -jnp.inf)
    top = s.max(axis=-1, keepdims=True)
    w = jnp.exp2((s - top) * SCALE2)
    total = w.sum(axis=-1, keepdims=True)
    out = jnp.dot(
        w.astype(jnp.bfloat16), v_ref[:, 0].reshape(size, DH), preferred_element_type=jnp.float32
    )
    o_ref[...] = (out / total).astype(jnp.bfloat16).reshape(frames, tokens, DH)


def attend_frames(trio):
    frames, _, rows, _ = trio.shape
    tokens = 32

    def part(n):
        return pl.BlockSpec((frames, 1, tokens, DH), lambda i: (0, n, i, 0))

    return pl.pallas_call(
        frames_body,
        grid=(rows // tokens,),
        out_shape=jax.ShapeDtypeStruct((frames, rows, DH), jnp.bfloat16),
        in_specs=[part(0), part(1), part(2)],
        out_specs=pl.BlockSpec((frames, tokens, DH), lambda i: (0, i, 0)),
        compiler_params=PARAMS,
        cost_estimate=COST,
    )(trio, trio, trio)


def over(axis, array):
    return lax.cond(
        lax.axis_index("dp") < 8,
        lambda a: lax.all_to_all(a, axis, split_axis=0, concat_axis=0, tiled=True),
        lambda a: a,
        array,
    )


def across(array):
    return lax.ppermute(array, "zh", [(0, 1), (1, 0)])


def on_device(q, k, v):
    rows, width = q.shape[1], q.shape[2]
    half = lax.axis_index("zh").astype(jnp.int32).reshape(1)
    (raw,) = pack(
        half,
        [(a, (3, -1)) for a in (q, k, v)],
        [(Y, 3, rows, DH)],
        [(n, y, 0, (y, n)) for n in range(3) for y in range(Y)],
    )
    far_raw = across(raw)
    more, trio = pack(
        half,
        [(a, (j, 0)) for j in range(2) for a in (k, v)]
        + [(q, (j, 0)) for j in range(2)]
        + [(a, (2, 1)) for a in (q, k, v)]
        + [(a, (HS // Y + g, 0)) for g in range(HT // Y) for a in (q, k, v)],
        [(Y, 9, rows, DH), (HT, 3, rows, DH)],
        [(n, y, 0, (y, n)) for n in range(9) for y in range(Y)]
        + [
            (9 + g * 3 + a, y, 1, (g * Y + y, a))
            for g in range(HT // Y)
            for a in range(3)
            for y in range(Y)
        ],
        (raw,),
    )
    mixed = over("y", more)
    far0 = across(take(mixed, 0, 2))
    trio = over("tm", trio)
    far1 = across(take(mixed, 2, 2, (trio,)))
    frames_out = over("tm", attend_frames(trio))
    early = unpack([frames_out], [(0, h) for h in range(HT)], HS, rows, width)
    far = over("y", far_raw)
    own = over(
        "y",
        attend(
            [((mixed, 6), (mixed, 7), (far, 1)), ((far, 0), (mixed, 7), (far, 1))], 2, after=(early,)
        ),
    )
    back = across(own[:, 1])
    pairs = attend([((mixed, 4), (mixed, 0), (far0, 0))], 2, after=(own,))
    pairs = over("y", attend([((mixed, 5), (mixed, 2), (far1, 0))], 2, 1, pairs))
    return unpack(
        [pairs, own, back],
        [(0, (y, j)) for j in range(2) for y in range(Y)]
        + [((1, (y, 0)), (2, y)) for y in range(Y)]
        + [((2, y), (1, (y, 0))) for y in range(Y)],
        0,
        rows,
        width,
        early,
        LAST,
    )


def solution(mesh):
    fine = Mesh(mesh.devices.reshape(8, 8, Y, 2), ("dp", "tm", "y", "zh"))
    spec = P(("dp", "tm"), ("y", "zh"), None)
    return jax.shard_map(
        on_device, mesh=fine, in_specs=(spec, spec, spec), out_specs=spec, check_vma=False
    )
```

```python
import functools
import math

import jax
import jax.numpy as jnp
from jax import lax
from jax.experimental import pallas as pl
from jax.experimental.pallas import tpu as pltpu
from jax.sharding import Mesh, PartitionSpec as P

HS = 16
HT = 8
DH = 128
Y = 4
SCALE = 1.0 / math.sqrt(DH)
SCALE2 = SCALE * math.log2(math.e)
ANY = pl.BlockSpec(memory_space=pl.ANY)
PARAMS = pltpu.CompilerParams(vmem_limit_bytes=60 * 1024 * 1024)
COST = pl.CostEstimate(flops=0, bytes_accessed=0, transcendentals=0)


def whole(shape):
    return pl.BlockSpec(shape, lambda *_: (0,) * len(shape))


def pack(half, sources, out_shapes, plan, after=()):
    rows, count, skip = sources[0][0].shape[1], len(sources), len(after)

    def body(half_ref, *refs):
        for source, y, o, index in plan:
            refs[count + skip + o][index] = refs[source][0, :, pl.ds(y * DH, DH)]

    def column(group):
        return lambda i, half_ref: (0, 0, group[0] + group[1] * half_ref[0])

    return pl.pallas_call(
        body,
        grid_spec=pltpu.PrefetchScalarGridSpec(
            num_scalar_prefetch=1,
            grid=(1,),
            in_specs=[pl.BlockSpec((1, rows, Y * DH), column(g)) for _, g in sources] + [ANY] * skip,
            out_specs=[whole(s) for s in out_shapes],
        ),
        out_shape=[jax.ShapeDtypeStruct(s, jnp.bfloat16) for s in out_shapes],
        compiler_params=PARAMS,
        cost_estimate=COST,
    )(half, *[array for array, _ in sources], *after)


def unpack(half, pieces, plan, rows, width, base=None):
    count = len(pieces)
    extra = [] if base is None else [base]

    def column(i, half_ref):
        place = jnp.int32(0)
        for n, ((a, b), _) in enumerate(plan):
            place = jnp.where(i == n, a + b * half_ref[0], place)
        return (0, 0, place)

    def body(half_ref, *refs):
        out = refs[count + len(extra)]
        for n, (_, heads) in enumerate(plan):

            @pl.when(pl.program_id(0) == n)
            def _write(heads=heads):
                for y, (p, index) in enumerate(heads):
                    out[0, :, pl.ds(y * DH, DH)] = refs[p][index]

    return pl.pallas_call(
        body,
        grid_spec=pltpu.PrefetchScalarGridSpec(
            num_scalar_prefetch=1,
            grid=(len(plan),),
            in_specs=[whole(p.shape) for p in pieces] + [ANY] * len(extra),
            out_specs=pl.BlockSpec((1, rows, Y * DH), column),
        ),
        out_shape=jax.ShapeDtypeStruct((1, rows, width), jnp.bfloat16),
        input_output_aliases={1 + count: 0} if extra else {},
        compiler_params=PARAMS,
        cost_estimate=COST,
    )(half, *pieces, *extra)


def scores_of(q, k):
    return lax.dot_general(q, k, (((1,), (1,)), ((), ())), preferred_element_type=jnp.float32)


def attend_body(jobs, *refs):
    o_ref = refs[-1]
    _, _, rows, _ = o_ref.shape
    size, parts = Y * rows, 2
    step = size // parts

    def flat(n):
        return refs[n][...].reshape(size, DH)

    def scores(task):
        q, kl, _, kr, _ = jobs[task // parts]
        query = flat(q)[task % parts * step : (task % parts + 1) * step]
        return scores_of(query, flat(kl)), scores_of(query, flat(kr))

    def weigh(w, n):
        both = jnp.concatenate([flat(n), jnp.ones((size, DH), jnp.bfloat16)], axis=-1)
        return jnp.dot(w.astype(jnp.bfloat16), both, preferred_element_type=jnp.float32)

    tasks = len(jobs) * parts
    ahead, outs = scores(0), []
    for task in range(tasks):
        (sl, sr), ahead = ahead, scores(task + 1) if task + 1 < tasks else None
        top = jnp.maximum(sl.max(axis=-1, keepdims=True), sr.max(axis=-1, keepdims=True))
        _, _, vl, _, vr = jobs[task // parts]
        out = weigh(jnp.exp2((sl - top) * SCALE2), vl) + weigh(jnp.exp2((sr - top) * SCALE2), vr)
        outs.append((out[:, :DH] / out[:, DH:]).astype(jnp.bfloat16))
    for n in range(len(jobs)):
        o_ref[:, n] = jnp.concatenate(outs[n * parts : (n + 1) * parts]).reshape(Y, rows, DH)


def attend(jobs, slots, slot=0, base=None, after=()):
    operands, indices = [], []

    def use(array, n):
        for m, (other, k) in enumerate(operands):
            if other is array and k == n:
                return m
        operands.append((array, n))
        return len(operands) - 1

    for (q, sq), (near, sn), (far, sf) in jobs:
        indices.append((use(q, sq), use(near, sn), use(near, sn + 1), use(far, sf), use(far, sf + 1)))
    rows = jobs[0][0][0].shape[2]
    extra = [] if base is None else [base]
    return pl.pallas_call(
        functools.partial(attend_body, indices),
        grid=(1,),
        out_shape=jax.ShapeDtypeStruct((Y, slots, rows, DH), jnp.bfloat16),
        in_specs=[
            pl.BlockSpec((Y, 1, rows, DH), lambda i, n=n: (0, n, 0, 0)) for _, n in operands
        ]
        + [ANY] * (len(extra) + len(after)),
        out_specs=pl.BlockSpec(
            (Y, len(jobs), rows, DH), lambda i: (0, slot // len(jobs), 0, 0)
        ),
        input_output_aliases={len(operands): 0} if extra else {},
        compiler_params=PARAMS,
        cost_estimate=COST,
    )(*[array for array, _ in operands], *extra, *after)


def take(array, first, count, after=()):
    _, _, rows, _ = array.shape

    def body(i_ref, *refs):
        refs[-1][...] = i_ref[...]

    return pl.pallas_call(
        body,
        grid=(Y,),
        out_shape=jax.ShapeDtypeStruct((Y, count, rows, DH), jnp.bfloat16),
        in_specs=[pl.BlockSpec((1, count, rows, DH), lambda i: (i, first // count, 0, 0))]
        + [ANY] * len(after),
        out_specs=pl.BlockSpec((1, count, rows, DH), lambda i: (i, 0, 0, 0)),
        compiler_params=PARAMS,
        cost_estimate=COST,
    )(array, *after)


def frames_body(q_ref, k_ref, v_ref, o_ref):
    frames, _, tokens, _ = q_ref.shape
    size = frames * tokens
    s = scores_of(q_ref[:, 0].reshape(size, DH), k_ref[:, 0].reshape(size, DH))
    row = lax.broadcasted_iota(jnp.int32, (size, size), 0)
    column = lax.broadcasted_iota(jnp.int32, (size, size), 1)
    same = (row & (tokens - 1)) == (column & (tokens - 1))
    s = jnp.where(same, s, -jnp.inf)
    top = s.max(axis=-1, keepdims=True)
    w = jnp.exp2((s - top) * SCALE2)
    total = w.sum(axis=-1, keepdims=True)
    out = jnp.dot(
        w.astype(jnp.bfloat16), v_ref[:, 0].reshape(size, DH), preferred_element_type=jnp.float32
    )
    o_ref[...] = (out / total).astype(jnp.bfloat16).reshape(frames, tokens, DH)


def attend_frames(trio):
    frames, _, rows, _ = trio.shape
    tokens = 32

    def part(n):
        return pl.BlockSpec((frames, 1, tokens, DH), lambda i: (0, n, i, 0))

    return pl.pallas_call(
        frames_body,
        grid=(rows // tokens,),
        out_shape=jax.ShapeDtypeStruct((frames, rows, DH), jnp.bfloat16),
        in_specs=[part(0), part(1), part(2)],
        out_specs=pl.BlockSpec((frames, tokens, DH), lambda i: (0, i, 0)),
        compiler_params=PARAMS,
        cost_estimate=COST,
    )(trio, trio, trio)


def over(axis, array):
    return lax.cond(
        lax.axis_index("dp") < 8,
        lambda a: lax.all_to_all(a, axis, split_axis=0, concat_axis=0, tiled=True),
        lambda a: a,
        array,
    )


def across(array):
    return lax.ppermute(array, "zh", [(0, 1), (1, 0)])


def on_device(q, k, v):
    rows, width = q.shape[1], q.shape[2]
    half = lax.axis_index("zh").astype(jnp.int32).reshape(1)
    (raw,) = pack(
        half,
        [(a, (3, -1)) for a in (q, k, v)],
        [(Y, 3, rows, DH)],
        [(n, y, 0, (y, n)) for n in range(3) for y in range(Y)],
    )
    far_raw = across(raw)
    more, trio = pack(
        half,
        [(a, (j, 0)) for j in range(2) for a in (k, v)]
        + [(q, (j, 0)) for j in range(2)]
        + [(a, (2, 1)) for a in (q, k, v)]
        + [(a, (HS // Y + g, 0)) for g in range(HT // Y) for a in (q, k, v)],
        [(Y, 9, rows, DH), (HT, 3, rows, DH)],
        [(n, y, 0, (y, n)) for n in range(9) for y in range(Y)]
        + [
            (9 + g * 3 + a, y, 1, (g * Y + y, a))
            for g in range(HT // Y)
            for a in range(3)
            for y in range(Y)
        ],
        (raw,),
    )
    mixed = over("y", more)
    far0 = across(take(mixed, 0, 2))
    trio = over("tm", trio)
    far1 = across(take(mixed, 2, 2, (trio,)))
    frames_out = over("tm", attend_frames(trio))
    early = unpack(
        half,
        [frames_out],
        [((HS // Y + g, 0), [(0, g * Y + y) for y in range(Y)]) for g in range(HT // Y)],
        rows,
        width,
    )
    far = over("y", far_raw)
    own = over(
        "y",
        attend(
            [((mixed, 6), (mixed, 7), (far, 1)), ((far, 0), (mixed, 7), (far, 1))], 2, after=(frames_out,)
        ),
    )
    back = across(own[:, 1])
    pairs = attend([((mixed, 4), (mixed, 0), (far0, 0))], 2, after=(own, early))
    pairs = over("y", attend([((mixed, 5), (mixed, 2), (far1, 0))], 2, 1, pairs))
    return unpack(
        half,
        [pairs, own, back],
        [((j, 0), [(0, (y, j)) for y in range(Y)]) for j in range(2)]
        + [((2, 1), [(1, (y, 0)) for y in range(Y)]), ((3, -1), [(2, y) for y in range(Y)])],
        rows,
        width,
        early,
    )


def solution(mesh):
    fine = Mesh(mesh.devices.reshape(8, 8, Y, 2), ("dp", "tm", "y", "zh"))
    spec = P(("dp", "tm"), ("y", "zh"), None)
    return jax.shard_map(
        on_device, mesh=fine, in_specs=(spec, spec, spec), out_specs=spec, check_vma=False
    )
```
